32 devices in a mesh: groups: 2 (over x), tile: 16 (over z, y, core).
Axes of the slice: x: 2, y: 2, z: 4, core: 2. Of those that a mesh axis runs over, the one named last changes fastest.
Arguments:
- object_slices: float32 [3, 2, 4096, 512], P(None, None, ('groups', 'tile')), parts along dimension 2, may hold values from -1 to 1.3
- probe: float32 [4, 128, 128], P('groups'), parts along dimension 0, may hold values from -4.2 to 4.2
- propagator_phase: float32 [128, 128], replicated, may hold values from -3.140625 to 3.140625
- intensity: float32 [256, 128, 128], P(('groups', 'tile')), parts along dimension 0, may hold values from 0.1 to 3
- scan_rows: int32 [256], P(('groups', 'tile')), parts along dimension 0, may hold values from -32 to 32
- scan_cols: int32 [256], P(('groups', 'tile')), parts along dimension 0, may hold values from 0 to 384
Outputs:
- object_grad: float32 [3, 2, 4096, 512], P(None, None, ('groups', 'tile')), parts along dimension 2
- probe_grad: float32 [4, 128, 128], P('groups'), parts along dimension 0
The draws below stay inside these ranges and needn't reach their ends.
There are 2 independent parts, one for each index of `groups`. The reference program is written for one: setup_inputs(seed, part) draws one part's arguments, and reference() takes and returns one part's arrays. A program takes and returns all parts, laid end to end along the dimension named above; an argument that names none is the same for every part. Nothing has to cross between parts.
All inputs are finite; a program needn't handle non-finite values.
Results may differ from the reference program's by a relative error of at most 0.0003.
Values sent between devices are 32-bit elements; how exact they have to be, the bound alone decides.
A program may use at most 64 MiB of HBM per device.

```python
import math
import jax
import jax.numpy as jnp
from jax import lax

PS = 128
SLICES = 3
TR = 128
NYW = 512
HALO = 32
POS_DEV = 8
POSITIONS = 128
NX = 2048


def set_ends(entries, stream_key, low, top_value):
    longest = entries.shape.index(max(entries.shape))
    spots = []
    for shift in (0, 1):
        where = [jax.random.randint(jax.random.fold_in(stream_key, axis), (), 0, length) for axis, length in enumerate(entries.shape)]
        where[longest] = (where[longest] + shift) % entries.shape[longest]
        spots.append(tuple(where))
    return entries.at[spots[0]].set(low).at[spots[1]].set(top_value)


def levels(own_key, shape, pieces, low, high):
    def one(dim, shards_of):
        heights = jax.random.uniform(jax.random.fold_in(jax.random.fold_in(own_key, 6), dim), (shards_of,), jnp.float32, low / len(pieces), high / len(pieces))
        return jnp.repeat(jnp.exp(heights), shape[dim] // shards_of).reshape((-1,) + (1,) * (len(shape) - dim - 1))

    gain = one(*pieces[0])
    for cut in pieces[1:]:
        gain = gain * one(*cut)
    return gain


def gaussian(key, shape, scale, most, held_as=jnp.bfloat16):
    return jnp.clip(scale * jax.random.normal(key, shape, jnp.float32), -most, most).astype(held_as)


def setup_inputs(seed: int = 0, part: int = 0) -> dict:
    keys = jax.random.split(jax.random.key(seed), 7)
    own_keys = jax.random.split(jax.random.fold_in(keys[6], part), 7)
    return {
        "object_slices": jnp.clip(-1.0 + 2.3 * jax.random.uniform(own_keys[0], (SLICES, 2, NX, NYW), jnp.float32) ** levels(own_keys[0], (SLICES, 2, NX, NYW), ((2, 16),), -0.2, 0.2), -1.0, 1.3),
        "probe": gaussian(own_keys[1], (2, PS, PS), 0.7, 4.2, jnp.float32),
        "propagator_phase": jnp.clip(jax.random.uniform(keys[2], (PS, PS), jnp.float32, -3.140625, 3.140625), -3.140625, 3.140625),
        "intensity": jnp.clip(jnp.exp(math.log(3.0) - 3.4011974 * jax.random.uniform(own_keys[3], (POSITIONS, PS, PS), jnp.float32) ** levels(own_keys[3], (POSITIONS, PS, PS), ((0, 16),), -0.2, 0.2)), 0.1, 3.0),
        "scan_rows": set_ends(jax.random.randint(own_keys[4], (POSITIONS,), 0 - HALO, TR + HALO - PS + 1), jax.random.fold_in(own_keys[4], 1), 0 - HALO, TR + HALO - PS).astype(jnp.int32),
        "scan_cols": set_ends(jax.random.randint(own_keys[5], (POSITIONS,), 0, NYW - PS + 1), jax.random.fold_in(own_keys[5], 1), 0, NYW - PS).astype(jnp.int32),
    }


def position_loss(patch, probe, propagator, image):
    wave = lax.complex(probe[0], probe[1])
    kernel = lax.complex(propagator[0], propagator[1])
    layers = patch.shape[0]
    for layer in range(layers):
        wave = wave * lax.complex(patch[layer, 0], patch[layer, 1])
        if layer + 1 < layers:
            spectrum = jnp.fft.fft2(wave, norm='ortho')
            wave = jnp.fft.ifft2(kernel * spectrum, norm='ortho')
    exit_wave = jnp.fft.fft2(wave, norm='ortho')
    far_re = jnp.real(exit_wave)
    far_im = jnp.imag(exit_wave)
    excess = far_re * far_re + far_im * far_im - image
    return jnp.sum(excess * excess)

def reference(object_slices, probe, propagator_phase, intensity, scan_rows, scan_cols):
    propagator = jnp.stack([jnp.cos(propagator_phase), jnp.sin(propagator_phase)])
    positions = scan_rows.shape[0]
    owner = jnp.arange(positions, dtype=jnp.int32) // POS_DEV
    tops = (owner * TR + scan_rows) % NX
    offsets = jnp.arange(PS, dtype=jnp.int32)
    gradient_fn = jax.grad(position_loss, argnums=(0, 1))

    def visit(carry, item):
        accum, probe_acc = carry
        top, left, image = item
        row_index = ((top + offsets) % NX).astype(jnp.int32)
        col_index = (left + offsets).astype(jnp.int32)
        patch = object_slices[:, :, row_index[:, None], col_index[None, :]]
        grad_patch, grad_probe = gradient_fn(patch, probe, propagator, image)
        accum = accum.at[:, :, row_index[:, None], col_index[None, :]].add(grad_patch)
        return ((accum, probe_acc + grad_probe), None)
    start = (jnp.zeros_like(object_slices), jnp.zeros_like(probe))
    (object_grad, probe_total), _ = lax.scan(visit, start, (tops, scan_cols, intensity))
    return (object_grad, probe_total / math.sqrt(positions))
```

```python
import functools
import math

import jax
import jax.numpy as jnp
import ml_dtypes
import numpy as np
from jax import lax
from jax.experimental import pallas as pl
from jax.experimental.pallas import tpu as pltpu
from jax.sharding import PartitionSpec as P

HALO = 32
BF = jnp.bfloat16
F32 = jnp.float32


def dft_tables(n):
    k = np.arange(n)
    angle = -2.0 * math.pi * (k[:, None] * k[None, :] % n) / n
    re, im = np.cos(angle) / math.sqrt(n), np.sin(angle) / math.sqrt(n)
    a = np.block([[re, im], [-im, re]])

    def parts(m):
        hi = m.astype(ml_dtypes.bfloat16)
        lo = (m - hi.astype(np.float64)).astype(ml_dtypes.bfloat16)
        return hi, lo

    ahi, alo = parts(a)
    thi, tlo = parts(a.T)
    right = np.stack([np.concatenate([ahi, ahi, alo], 0), np.concatenate([thi, thi, tlo], 0)])
    left = np.stack([np.concatenate([thi, thi, tlo], 1), np.concatenate([ahi, ahi, alo], 1)])
    return right, left


def split(x):
    hi = x.astype(BF)
    lo = (x - hi.astype(F32)).astype(BF)
    return hi, lo


def rmul(x, right):
    hi, lo = split(x)
    return jnp.dot(jnp.concatenate([hi, lo, hi], axis=1), right, preferred_element_type=F32)


def lmul(x, left):
    hi, lo = split(x)
    return jnp.dot(left, jnp.concatenate([hi, lo, hi], axis=0), preferred_element_type=F32)


def flip(x, n):
    return jnp.concatenate(
        [
            jnp.concatenate([x[:n, :n], x[n:, :n]], axis=1),
            jnp.concatenate([x[:n, n:], x[n:, n:]], axis=1),
        ],
        axis=0,
    )


def cmul(ar, ai, br, bi):
    return ar * br - ai * bi, ar * bi + ai * br


def cmulc(ar, ai, br, bi):
    return ar * br + ai * bi, ai * br - ar * bi


def body(
    n, pairs, rows_ref, cols_ref, obj_ref, top_ref, bot_ref, probe_ref, ker_ref, img_ref, right_ref, left_ref,
    grad_ref, gtop_ref, gbot_ref, pg_ref, pad, acc, patch, psi,
):
    layers, _, own, width = obj_ref.shape
    blocks = width // n
    for b in range(blocks):
        cols = slice(b * n, (b + 1) * n)
        pad[:, :, b, :HALO] = top_ref[:, :, :, cols]
        pad[:, :, b, HALO : HALO + own] = obj_ref[:, :, :, cols]
        pad[:, :, b, HALO + own :] = bot_ref[:, :, :, cols]
    acc[...] = jnp.zeros_like(acc)
    pg_ref[...] = jnp.zeros_like(pg_ref)
    total = rows_ref.shape[0]

    def where(p):
        top = rows_ref[p] + HALO
        left = cols_ref[p]
        block = jnp.minimum(left // n, blocks - 2)
        return top, block, left - block * n

    def extract(p, s):
        top, block, off = where(p)
        shift = lax.rem(2 * n - off, 2 * n)
        for c in range(2):
            x = jnp.concatenate([pad[s, c, block + i, pl.ds(top, n), :] for i in range(2)], axis=1)
            patch[p, s, c] = pltpu.roll(x, shift, 1)[:, :n]

    def deposit(p, s, gr, gi):
        top, block, off = where(p)
        zero = jnp.zeros((n, n), F32)
        for c, g in enumerate((gr, gi)):
            v = pltpu.roll(jnp.concatenate([g, zero], axis=1), off, 1)
            acc[s, c, block, pl.ds(top, n), :] += v[:, :n]
            acc[s, c, block + 1, pl.ds(top, n), :] += v[:, n:]

    def join(waves):
        return jnp.concatenate([jnp.concatenate(w, axis=1) for w in waves], axis=0)

    def parts(x):
        return [(x[:n, :n], x[:n, n:]), (x[n:, :n], x[n:, n:])]

    def transform(x, way):
        y = rmul(x, right_ref[way])
        return flip(lmul(flip(y, n), left_ref[way]), n)

    def transform_all(xs, way):
        ys = [rmul(x, right_ref[way]) for x in xs]
        zs = [lmul(flip(y, n), left_ref[way]) for y in ys]
        return [flip(z, n) for z in zs]

    def step(g, carry):
        groups = [[(g * pairs + i) * 2 + j for j in range(2)] for i in range(pairs)]
        for s in range(layers):
            for group in groups:
                for p in group:
                    extract(p, s)
        waves = [[(probe_ref[0], probe_ref[1]) for p in group] for group in groups]
        for s in range(layers):
            waves = [
                [cmul(*w, patch[p, s, 0], patch[p, s, 1]) for p, w in zip(group, ws)]
                for group, ws in zip(groups, waves)
            ]
            spec = transform_all([join(ws) for ws in waves], 0)
            if s + 1 < layers:
                spec = [join([cmul(*w, ker_ref[0], ker_ref[1]) for w in parts(x)]) for x in spec]
                waves = [parts(x) for x in transform_all(spec, 1)]
                for group, ws in zip(groups, waves):
                    for p, w in zip(group, ws):
                        psi[p, s, 0] = w[0]
                        psi[p, s, 1] = w[1]
        back = []
        for group, x in zip(groups, spec):
            out = []
            for p, (fr, fi) in zip(group, parts(x)):
                e = 4.0 * (fr * fr + fi * fi - img_ref[p])
                out.append((e * fr, e * fi))
            back.append(join(out))
        for s in reversed(range(layers)):
            back = transform_all(back, 1)
            nxt = []
            for group, x in zip(groups, back):
                out = []
                for p, w in zip(group, parts(x)):
                    if s:
                        inc = psi[p, s - 1, 0], psi[p, s - 1, 1]
                    else:
                        inc = probe_ref[0], probe_ref[1]
                    deposit(p, s, *cmulc(*w, *inc))
                    out.append(cmulc(*w, patch[p, s, 0], patch[p, s, 1]))
                nxt.append(out)
            if s:
                spec = transform_all([join(ws) for ws in nxt], 0)
                back = [join([cmulc(*w, ker_ref[0], ker_ref[1]) for w in parts(x)]) for x in spec]
        for ws in nxt:
            for w in ws:
                pg_ref[0] += w[0]
                pg_ref[1] += w[1]
        return carry

    lax.fori_loop(0, total // (2 * pairs), step, 0)
    for b in range(blocks):
        cols = slice(b * n, (b + 1) * n)
        gtop_ref[:, :, :, cols] = acc[:, :, b, :HALO]
        grad_ref[:, :, :, cols] = acc[:, :, b, HALO : HALO + own]
        gbot_ref[:, :, :, cols] = acc[:, :, b, HALO + own :]


def core(scan_rows, scan_cols, obj, top, bot, probe, ker, intensity, pairs=4):
    layers, _, own, width = obj.shape
    n = probe.shape[1]
    total = scan_rows.shape[0]
    right, left = dft_tables(n)
    vmem = pl.BlockSpec(memory_space=pltpu.VMEM)
    smem = pl.BlockSpec(memory_space=pltpu.SMEM)
    return pl.pallas_call(
        functools.partial(body, n, pairs),
        out_shape=[
            jax.ShapeDtypeStruct(obj.shape, F32),
            jax.ShapeDtypeStruct((layers, 2, HALO, width), F32),
            jax.ShapeDtypeStruct((layers, 2, HALO, width), F32),
            jax.ShapeDtypeStruct(probe.shape, F32),
        ],
        in_specs=[smem, smem] + [vmem] * 8,
        out_specs=[vmem] * 4,
        scratch_shapes=[
            pltpu.VMEM((layers, 2, width // n, own + 2 * HALO, n), F32),
            pltpu.VMEM((layers, 2, width // n, own + 2 * HALO, n), F32),
            pltpu.VMEM((total, layers, 2, n, n), F32),
            pltpu.VMEM((total, layers - 1, 2, n, n), F32),
        ],
        compiler_params=pltpu.CompilerParams(vmem_limit_bytes=48 * 1024 * 1024),
    )(scan_rows, scan_cols, obj, top, bot, probe, ker, intensity, jnp.asarray(right), jnp.asarray(left))


def down(count):
    return [(i, (i + 1) % count) for i in range(count)]


def up(count):
    return [((i + 1) % count, i) for i in range(count)]


def local(object_slices, probe, propagator_phase, intensity, scan_rows, scan_cols):
    count = lax.axis_size("tile")
    own = object_slices.shape[2]
    ker = jnp.stack([jnp.cos(propagator_phase), jnp.sin(propagator_phase)])
    top = lax.ppermute(object_slices[:, :, own - HALO :], "tile", down(count))
    bot = lax.ppermute(object_slices[:, :, :HALO], "tile", up(count))
    grad, gtop, gbot, pg = core(scan_rows, scan_cols, object_slices, top, bot, probe, ker, intensity)
    from_below = lax.ppermute(gtop, "tile", up(count))
    from_above = lax.ppermute(gbot, "tile", down(count))
    grad = grad.at[:, :, :HALO].add(from_above)
    grad = grad.at[:, :, own - HALO :].add(from_below)
    total = lax.psum(pg, "tile")
    return grad, total / math.sqrt(count * scan_rows.shape[0])


def solution(mesh):
    placed = (
        P(None, None, ("groups", "tile"), None),
        P("groups", None, None),
        P(),
        P(("groups", "tile"), None, None),
        P(("groups", "tile")),
        P(("groups", "tile")),
    )
    return jax.shard_map(
        local,
        mesh=mesh,
        in_specs=placed,
        out_specs=(P(None, None, ("groups", "tile"), None), P("groups", None, None)),
        check_vma=False,
    )
```

```python
import functools
import math

import jax
import jax.numpy as jnp
import ml_dtypes
import numpy as np
from jax import lax
from jax.experimental import pallas as pl
from jax.experimental.pallas import tpu as pltpu
from jax.sharding import PartitionSpec as P

HALO = 32
BF = jnp.bfloat16
F32 = jnp.float32


def dft_tables(n):
    k = np.arange(n)
    angle = -2.0 * math.pi * (k[:, None] * k[None, :] % n) / n
    re, im = np.cos(angle) / math.sqrt(n), np.sin(angle) / math.sqrt(n)
    a = np.block([[re, im], [-im, re]])

    def parts(m):
        hi = m.astype(ml_dtypes.bfloat16)
        lo = (m - hi.astype(np.float64)).astype(ml_dtypes.bfloat16)
        return hi, lo

    ahi, alo = parts(a)
    thi, tlo = parts(a.T)
    right = np.stack([np.concatenate([ahi, ahi, alo], 0), np.concatenate([thi, thi, tlo], 0)])
    left = np.stack([np.concatenate([thi, thi, tlo], 1), np.concatenate([ahi, ahi, alo], 1)])
    return right, left


def split(x):
    hi = x.astype(BF)
    lo = (x - hi.astype(F32)).astype(BF)
    return hi, lo


def rmul(x, right):
    hi, lo = split(x)
    return jnp.dot(jnp.concatenate([hi, lo, hi], axis=1), right, preferred_element_type=F32)


def lmul(x, left):
    hi, lo = split(x)
    return jnp.dot(left, jnp.concatenate([hi, lo, hi], axis=0), preferred_element_type=F32)


def flip(x, n):
    return jnp.concatenate(
        [
            jnp.concatenate([x[:n, :n], x[n:, :n]], axis=1),
            jnp.concatenate([x[:n, n:], x[n:, n:]], axis=1),
        ],
        axis=0,
    )


def cmul(ar, ai, br, bi):
    return ar * br - ai * bi, ar * bi + ai * br


def cmulc(ar, ai, br, bi):
    return ar * br + ai * bi, ai * br - ar * bi


def body(
    n, pairs, rows_ref, cols_ref, obj_ref, top_ref, bot_ref, probe_ref, ker_ref, img_ref, right_ref, left_ref,
    grad_ref, gtop_ref, gbot_ref, pg_ref, pad, acc, patch, psi,
):
    layers, _, own, width = obj_ref.shape
    blocks = width // n
    for b in range(blocks):
        cols = slice(b * n, (b + 1) * n)
        pad[:, :, b, :HALO] = top_ref[:, :, :, cols]
        pad[:, :, b, HALO : HALO + own] = obj_ref[:, :, :, cols]
        pad[:, :, b, HALO + own :] = bot_ref[:, :, :, cols]
    acc[...] = jnp.zeros_like(acc)
    pg_ref[...] = jnp.zeros_like(pg_ref)
    total = rows_ref.shape[0]

    def where(p):
        top = rows_ref[p] + HALO
        left = cols_ref[p]
        block = jnp.minimum(left // n, blocks - 2)
        return top, block, left - block * n

    def extract(p, s):
        top, block, off = where(p)
        shift = lax.rem(2 * n - off, 2 * n)
        for c in range(2):
            x = jnp.concatenate([pad[s, c, block + i, pl.ds(top, n), :] for i in range(2)], axis=1)
            patch[p, s, c] = pltpu.roll(x, shift, 1)[:, :n]

    def deposit(p, s, gr, gi):
        top, block, off = where(p)
        zero = jnp.zeros((n, n), F32)
        for c, g in enumerate((gr, gi)):
            v = pltpu.roll(jnp.concatenate([g, zero], axis=1), off, 1)
            acc[s, c, block, pl.ds(top, n), :] += v[:, :n]
            acc[s, c, block + 1, pl.ds(top, n), :] += v[:, n:]

    def join(waves):
        return jnp.concatenate([jnp.concatenate(w, axis=1) for w in waves], axis=0)

    def parts(x):
        return [(x[:n, :n], x[:n, n:]), (x[n:, :n], x[n:, n:])]

    def transform(x, way):
        y = rmul(x, right_ref[way])
        return flip(lmul(flip(y, n), left_ref[way]), n)

    def transform_all(xs, way):
        ys = [rmul(x, right_ref[way]) for x in xs]
        zs = [lmul(flip(y, n), left_ref[way]) for y in ys]
        return [flip(z, n) for z in zs]

    def step(g, carry):
        groups = [[(g * pairs + i) * 2 + j for j in range(2)] for i in range(pairs)]
        for s in range(layers):
            for group in groups:
                for p in group:
                    extract(p, s)
        waves = [[(probe_ref[0], probe_ref[1]) for p in group] for group in groups]
        for s in range(layers):
            waves = [
                [cmul(*w, patch[p, s, 0], patch[p, s, 1]) for p, w in zip(group, ws)]
                for group, ws in zip(groups, waves)
            ]
            spec = transform_all([join(ws) for ws in waves], 0)
            if s + 1 < layers:
                spec = [join([cmul(*w, ker_ref[0], ker_ref[1]) for w in parts(x)]) for x in spec]
                waves = [parts(x) for x in transform_all(spec, 1)]
                for group, ws in zip(groups, waves):
                    for p, w in zip(group, ws):
                        psi[p, s, 0] = w[0]
                        psi[p, s, 1] = w[1]
        back = []
        for group, x in zip(groups, spec):
            out = []
            for p, (fr, fi) in zip(group, parts(x)):
                e = 4.0 * (fr * fr + fi * fi - img_ref[p])
                out.append((e * fr, e * fi))
            back.append(join(out))
        for s in reversed(range(layers)):
            back = transform_all(back, 1)
            nxt = []
            for group, x in zip(groups, back):
                out = []
                for p, w in zip(group, parts(x)):
                    if s:
                        inc = psi[p, s - 1, 0], psi[p, s - 1, 1]
                    else:
                        inc = probe_ref[0], probe_ref[1]
                    deposit(p, s, *cmulc(*w, *inc))
                    out.append(cmulc(*w, patch[p, s, 0], patch[p, s, 1]))
                nxt.append(out)
            if s:
                spec = transform_all([join(ws) for ws in nxt], 0)
                back = [join([cmulc(*w, ker_ref[0], ker_ref[1]) for w in parts(x)]) for x in spec]
        for ws in nxt:
            for w in ws:
                pg_ref[0] += w[0]
                pg_ref[1] += w[1]
        return carry

    lax.fori_loop(0, total // (2 * pairs), step, 0)
    for b in range(blocks):
        cols = slice(b * n, (b + 1) * n)
        gtop_ref[:, :, :, cols] = acc[:, :, b, :HALO]
        grad_ref[:, :, :, cols] = acc[:, :, b, HALO : HALO + own]
        gbot_ref[:, :, :, cols] = acc[:, :, b, HALO + own :]


def core(scan_rows, scan_cols, obj, top, bot, probe, ker, intensity, pairs=4):
    layers, _, own, width = obj.shape
    n = probe.shape[1]
    total = scan_rows.shape[0]
    right, left = dft_tables(n)
    vmem = pl.BlockSpec(memory_space=pltpu.VMEM)
    smem = pl.BlockSpec(memory_space=pltpu.SMEM)
    return pl.pallas_call(
        functools.partial(body, n, pairs),
        out_shape=[
            jax.ShapeDtypeStruct(obj.shape, F32),
            jax.ShapeDtypeStruct((layers, 2, HALO, width), F32),
            jax.ShapeDtypeStruct((layers, 2, HALO, width), F32),
            jax.ShapeDtypeStruct(probe.shape, F32),
        ],
        in_specs=[smem, smem] + [vmem] * 8,
        out_specs=[vmem] * 4,
        scratch_shapes=[
            pltpu.VMEM((layers, 2, width // n, own + 2 * HALO, n), F32),
            pltpu.VMEM((layers, 2, width // n, own + 2 * HALO, n), F32),
            pltpu.VMEM((total, layers, 2, n, n), F32),
            pltpu.VMEM((total, layers - 1, 2, n, n), F32),
        ],
        compiler_params=pltpu.CompilerParams(vmem_limit_bytes=48 * 1024 * 1024),
    )(scan_rows, scan_cols, obj, top, bot, probe, ker, intensity, jnp.asarray(right), jnp.asarray(left))


def at(tile):
    return dict(device_id={"tile": tile}, device_id_type=pl.DeviceIdType.MESH)


def halo_body(count, obj_ref, phase_ref, top_ref, bot_ref, ker_ref, send, recv):
    own = obj_ref.shape[2]
    me = lax.axis_index("tile")
    after, before = lax.rem(me + 1, count), lax.rem(me + count - 1, count)
    barrier = pltpu.get_barrier_semaphore()
    for peer in (before, after):
        pl.semaphore_signal(barrier, inc=1, **at(peer))
    pl.semaphore_wait(barrier, 2)
    copies = [
        pltpu.make_async_remote_copy(
            src_ref=obj_ref.at[:, :, pl.ds(own - HALO, HALO)], dst_ref=top_ref,
            send_sem=send.at[0], recv_sem=recv.at[0], **at(after),
        ),
        pltpu.make_async_remote_copy(
            src_ref=obj_ref.at[:, :, pl.ds(0, HALO)], dst_ref=bot_ref,
            send_sem=send.at[1], recv_sem=recv.at[1], **at(before),
        ),
    ]
    for copy in copies:
        copy.start()
    ker_ref[0] = jnp.cos(phase_ref[...])
    ker_ref[1] = jnp.sin(phase_ref[...])
    for copy in copies:
        copy.wait()


def halo_exchange(obj, phase, count):
    layers, _, _, width = obj.shape
    edge = jax.ShapeDtypeStruct((layers, 2, HALO, width), F32)
    anywhere = pl.BlockSpec(memory_space=pl.ANY)
    vmem = pl.BlockSpec(memory_space=pltpu.VMEM)
    return pl.pallas_call(
        functools.partial(halo_body, count),
        out_shape=[edge, edge, jax.ShapeDtypeStruct((2,) + phase.shape, F32)],
        in_specs=[anywhere, vmem],
        out_specs=[vmem] * 3,
        scratch_shapes=[pltpu.SemaphoreType.DMA((2,)), pltpu.SemaphoreType.DMA((2,))],
        compiler_params=pltpu.CompilerParams(
            collective_id=0, has_side_effects=True, vmem_limit_bytes=8 * 1024 * 1024
        ),
    )(obj, phase)


def reduce_body(
    count, scale, grad_ref, gtop_ref, gbot_ref, pg_ref, out_ref, probe_ref,
    edge, parts, piece, esend, erecv, ssend, srecv, gsend, grecv,
):
    own = grad_ref.shape[2]
    me = lax.axis_index("tile")
    after, before = lax.rem(me + 1, count), lax.rem(me + count - 1, count)
    barrier = pltpu.get_barrier_semaphore()

    def greet(d, c):
        pl.semaphore_signal(barrier, inc=1, **at(lax.rem(me + d, count)))
        return c

    lax.fori_loop(1, count, greet, 0)
    pl.semaphore_wait(barrier, count - 1)

    def scatter(d):
        peer = lax.rem(me + d, count)
        return pltpu.make_async_remote_copy(
            src_ref=pg_ref.at[peer], dst_ref=parts.at[d], send_sem=ssend.at[d], recv_sem=srecv.at[d], **at(peer)
        )

    def gather(d, slot):
        peer = lax.rem(me + d, count)
        return pltpu.make_async_remote_copy(
            src_ref=piece, dst_ref=probe_ref.at[slot], send_sem=gsend.at[d], recv_sem=grecv.at[d], **at(peer)
        )

    def run(f):
        def go(d, c):
            f(d)
            return c

        lax.fori_loop(1, count, go, 0)

    run(lambda d: scatter(d).start())
    edges = [
        pltpu.make_async_remote_copy(
            src_ref=gbot_ref, dst_ref=edge.at[0], send_sem=esend.at[0], recv_sem=erecv.at[0], **at(after)
        ),
        pltpu.make_async_remote_copy(
            src_ref=gtop_ref, dst_ref=edge.at[1], send_sem=esend.at[1], recv_sem=erecv.at[1], **at(before)
        ),
    ]
    for copy in edges:
        copy.start()
    run(lambda d: scatter(d).wait_recv())

    def add(d, total):
        return total + parts[d]

    piece[...] = lax.fori_loop(1, count, add, pg_ref[me]) * scale
    run(lambda d: gather(d, me).start())
    probe_ref[me] = piece[...]
    out_ref[:, :, HALO : own - HALO] = grad_ref[:, :, HALO : own - HALO]
    for copy in edges:
        copy.wait_recv()
    out_ref[:, :, :HALO] = grad_ref[:, :, :HALO] + edge[0]
    out_ref[:, :, own - HALO :] = grad_ref[:, :, own - HALO :] + edge[1]
    run(lambda d: gather(d, lax.rem(me + count - d, count)).wait_recv())
    run(lambda d: scatter(d).wait_send())
    run(lambda d: gather(d, me).wait_send())
    for copy in edges:
        copy.wait_send()


def reduce_exchange(grad, gtop, gbot, pg, count, scale):
    vmem = pl.BlockSpec(memory_space=pltpu.VMEM)
    n = pg.shape[2]
    rows = pg.shape[0] * pg.shape[1] // count
    dma = pltpu.SemaphoreType.DMA
    out, probe = pl.pallas_call(
        functools.partial(reduce_body, count, scale),
        out_shape=[
            jax.ShapeDtypeStruct(grad.shape, F32),
            jax.ShapeDtypeStruct((count, rows, n), F32),
        ],
        in_specs=[vmem] * 4,
        out_specs=[vmem] * 2,
        scratch_shapes=[
            pltpu.VMEM((2,) + gtop.shape, F32),
            pltpu.VMEM((count, rows, n), F32),
            pltpu.VMEM((rows, n), F32),
            dma((2,)), dma((2,)), dma((count,)), dma((count,)), dma((count,)), dma((count,)),
        ],
        compiler_params=pltpu.CompilerParams(
            collective_id=1, has_side_effects=True, vmem_limit_bytes=24 * 1024 * 1024
        ),
    )(grad, gtop, gbot, pg.reshape(count, rows, n))
    return out, probe.reshape(pg.shape)


def local(object_slices, probe, propagator_phase, intensity, scan_rows, scan_cols):
    count = lax.axis_size("tile")
    top, bot, ker = halo_exchange(object_slices, propagator_phase, count)
    grad, gtop, gbot, pg = core(scan_rows, scan_cols, object_slices, top, bot, probe, ker, intensity)
    scale = 1.0 / math.sqrt(count * scan_rows.shape[0])
    return reduce_exchange(grad, gtop, gbot, pg, count, scale)


def solution(mesh):
    placed = (
        P(None, None, ("groups", "tile"), None),
        P("groups", None, None),
        P(),
        P(("groups", "tile"), None, None),
        P(("groups", "tile")),
        P(("groups", "tile")),
    )
    return jax.shard_map(
        local,
        mesh=mesh,
        in_specs=placed,
        out_specs=(P(None, None, ("groups", "tile"), None), P("groups", None, None)),
        check_vma=False,
    )
```
